32 devices in a mesh: rows: 8 (over z, x), cols: 4 (over y, core).
Axes of the slice: x: 2, y: 2, z: 4, core: 2. Of those that a mesh axis runs over, the one named last changes fastest.
Arguments:
- points: float32 [24576, 1024], P('rows', 'cols'), may hold values from -80 to 80
- codes: int32 [128, 24576], P('cols', 'rows'), may hold values from 0 to 255, as said below
- rotation: float32 [1024, 1024], P('rows', 'cols'), may hold values from -0.16 to 1.16
Outputs:
- new_rotation: float32 [1024, 1024], P('rows', 'cols')
- centroids: float32 [128, 2048], P('cols')
The draws below stay inside these ranges and needn't reach their ends.
Inputs may be any that keep to these rules, and one draw needn't show every extreme that they name: For every subspace, the first 256 vectors hold each of the 256 codes once.
All inputs are finite; a program needn't handle non-finite values.
Results may differ from the reference program's by a relative error of at most 0.00011.
Values sent between devices are 32-bit elements; how exact they have to be, the bound alone decides.
A program may use at most 128 MiB of HBM per device.

```python
import jax
import jax.numpy as jnp
from jax import lax

D = 1024
M = 128
K = 256
NS_ITERS = 6
SUB = 8
TOTAL = 24576


def shared_codes(key):
    base = jax.random.fold_in(key, 11)
    key_raw, key_offset = jax.random.split(base)
    position = jnp.arange(TOTAL, dtype=jnp.int32)
    spread = K - 2 * K // 3 * position // TOTAL
    raw_codes = jax.random.randint(key_raw, (M, TOTAL), 0, 1 << 20, dtype=jnp.int32)
    drawn = raw_codes % spread[None, :]
    offsets = jax.random.randint(key_offset, (M, 1), 0, K, dtype=jnp.int32)
    cyclic = (position[None, :] + offsets) % K
    return jnp.where(position[None, :] < K, cyclic, drawn).astype(jnp.int32)


def draw_codes(key, part):
    return shared_codes(key)


def draw_points(key, part):
    code_table = shared_codes(key)
    table = jnp.clip(jax.random.normal(jax.random.fold_in(key, 12), (M, K, SUB), jnp.float32), -5.0, 5.0)
    centers = table[jnp.arange(M)[:, None], code_table]
    centers = centers.transpose(1, 0, 2).reshape(TOTAL, D)
    noise = jnp.clip(jax.random.normal(jax.random.fold_in(key, 14), (TOTAL, D), jnp.float32), -5.0, 5.0)
    unit = jax.random.uniform(jax.random.fold_in(key, 13), (D,), jnp.float32)
    feature_scale = jnp.exp(unit * jnp.log(3.0))
    return ((centers + 0.6 * noise) * feature_scale[None, :]).astype(jnp.float32)


def draw_rotation(key, part):
    noise = jnp.clip(jax.random.normal(jax.random.fold_in(key, 15), (D, D), jnp.float32), -5.0, 5.0)
    index_range = jnp.arange(D, dtype=jnp.int32)
    identity = (index_range[:, None] == index_range[None, :]).astype(jnp.float32)
    spread = 0.35
    return (identity + spread * noise / D ** 0.5).astype(jnp.float32)


def setup_inputs(seed: int = 0) -> dict:
    splits = jax.random.split(jax.random.key(seed), 4)
    return {
        "points": draw_points(jax.random.fold_in(splits[3], 71), 0),
        "codes": draw_codes(jax.random.fold_in(splits[3], 71), 0),
        "rotation": draw_rotation(jax.random.fold_in(splits[3], 71), 0),
    }


def reference(points, codes, rotation):
    highest = lax.Precision.HIGHEST
    rotated = jnp.dot(points, rotation, precision=highest, preferred_element_type=jnp.float32)
    blocks = rotated.reshape(TOTAL, M, SUB).transpose(1, 0, 2)

    def one_subspace(item):
        block, code_row = item
        sums_here = jax.ops.segment_sum(block, code_row, K)
        counts_here = jax.ops.segment_sum(jnp.ones((TOTAL,), jnp.float32), code_row, K)
        centers = sums_here / counts_here[:, None]
        return (centers, centers[code_row])
    centers_all, recon_all = lax.map(one_subspace, (blocks, codes))
    approx = recon_all.transpose(1, 0, 2).reshape(TOTAL, D)
    cross = jnp.dot(points.T, approx, precision=highest, preferred_element_type=jnp.float32)
    iterate = 1.7 * cross / jnp.sqrt(jnp.sum(cross * cross) + 1e-06)
    for step_index in range(NS_ITERS):
        gram = jnp.dot(iterate.T, iterate, precision=highest, preferred_element_type=jnp.float32)
        iterate = 1.5 * iterate - 0.5 * jnp.dot(iterate, gram, precision=highest, preferred_element_type=jnp.float32)
    new_rotation = iterate * D ** 0.5
    return (new_rotation, centers_all.reshape(M, K * SUB))
```

```python
import functools

import jax
import jax.numpy as jnp
from jax import lax
from jax.experimental import pallas as pl
from jax.experimental.pallas import tpu as pltpu
from jax.sharding import PartitionSpec as P

K = 256
NS_ITERS = 6
SUB = 8
LOW = 64
HIGH = K // LOW
GROUP = 4
F32 = jnp.float32
BF16 = jnp.bfloat16
MESH = pl.DeviceIdType.MESH
NT = (((1,), (1,)), ((), ()))
VMEM_BYTES = 56 * 1024 * 1024


def split(x):
    hi = x.astype(BF16)
    return hi, (x - hi.astype(F32)).astype(BF16)


def dot(left, right, dims):
    return lax.dot_general(left, right, dims, preferred_element_type=F32)


def dot3(left, right, dims):
    lh, ll = left
    rh, rl = right
    return dot(lh, rh, dims) + (dot(lh, rl, dims) + dot(ll, rh, dims))


def code_sums_kernel(codes_ref, rot_ref, sums_ref, counts_ref, left, right):
    n = codes_ref.shape[1]
    low_iota = lax.broadcasted_iota(jnp.int32, (LOW, n), 0)
    q_iota = lax.broadcasted_iota(jnp.int32, (8, n), 0)
    for g in range(codes_ref.shape[0] // GROUP):
        for i in range(GROUP):
            m = g * GROUP + i
            code = codes_ref[m : m + 1, :]
            q = code // LOW
            low = code - q * LOW
            right[i * LOW : (i + 1) * LOW, :] = jnp.where(low == low_iota, 1.0, 0.0).astype(BF16)
            value = rot_ref[m * SUB : (m + 1) * SUB, :]
            hi = value.astype(BF16).astype(F32)
            both = jnp.concatenate([hi, value - hi], axis=0)
            for h in range(HIGH):
                row = (i * HIGH + h) * 2 * SUB
                left[row : row + 2 * SUB, :] = jnp.where(q == h, both, 0.0).astype(BF16)
        for pair in range(GROUP // 2):
            row = 2 * SUB * HIGH * GROUP + pair * 16
            parts = []
            for i in range(2):
                m = g * GROUP + pair * 2 + i
                q = codes_ref[m : m + 1, :] // LOW
                parts.append(jnp.where(q == q_iota, 1.0, 0.0))
            left[row : row + 16, :] = jnp.concatenate(parts, axis=0).astype(BF16)
        out = dot(left[...], right[...], NT)
        for i in range(GROUP):
            m = g * GROUP + i
            lanes = slice(i * LOW, (i + 1) * LOW)
            pieces = []
            for h in range(HIGH):
                row = (i * HIGH + h) * 2 * SUB
                pieces.append(out[row : row + SUB, lanes] + out[row + SUB : row + 2 * SUB, lanes])
            sums_ref[m * SUB : (m + 1) * SUB, :] = jnp.concatenate(pieces, axis=1)
            row = 2 * SUB * HIGH * GROUP + i * 8
            counts_ref[m : m + 1, :] = jnp.concatenate(
                [out[row + h : row + h + 1, lanes] for h in range(HIGH)], axis=1
            )


def code_sums(codes, rot):
    subspaces, n = codes.shape
    block = 8
    rows = 2 * SUB * HIGH * GROUP + 8 * GROUP
    return pl.pallas_call(
        code_sums_kernel,
        grid=(subspaces // block,),
        in_specs=[
            pl.BlockSpec((block, n), lambda i: (i, 0)),
            pl.BlockSpec((block * SUB, n), lambda i: (i, 0)),
        ],
        out_specs=[
            pl.BlockSpec((block * SUB, K), lambda i: (i, 0)),
            pl.BlockSpec((block, K), lambda i: (i, 0)),
        ],
        out_shape=[
            jax.ShapeDtypeStruct((subspaces * SUB, K), F32),
            jax.ShapeDtypeStruct((subspaces, K), F32),
        ],
        scratch_shapes=[pltpu.VMEM((rows, n), BF16), pltpu.VMEM((GROUP * LOW, n), BF16)],
        compiler_params=pltpu.CompilerParams(vmem_limit_bytes=VMEM_BYTES),
        name="code_sums",
    )(codes, rot)


def cross_kernel(codes_ref, table_ref, points_ref, cross_ref, approx, phi, plo):
    subspaces, n = codes_ref.shape

    @pl.when(pl.program_id(0) == 0)
    def _():
        hi, lo = split(points_ref[...].T)
        phi[...] = hi
        plo[...] = lo

    for m in range(subspaces):
        rows = slice(m * SUB, (m + 1) * SUB)
        first = table_ref[rows, :128]
        second = table_ref[rows, 128:]
        for j in range(n // 128):
            lanes = slice(j * 128, (j + 1) * 128)
            code = jnp.broadcast_to(codes_ref[m : m + 1, lanes], (SUB, 128))
            inner = jnp.bitwise_and(code, 127)
            a = jnp.take_along_axis(first, inner, axis=1)
            b = jnp.take_along_axis(second, inner, axis=1)
            approx[rows, lanes] = jnp.where(code >= 128, b, a)
    cross_ref[...] = dot3((phi[...], plo[...]), split(approx[...]), NT)


def cross_terms(codes, table, points):
    subspaces, n = codes.shape
    d = points.shape[1]
    block = 32
    return pl.pallas_call(
        cross_kernel,
        grid=(subspaces // block,),
        in_specs=[
            pl.BlockSpec((block, n), lambda i: (i, 0)),
            pl.BlockSpec((block * SUB, K), lambda i: (i, 0)),
            pl.BlockSpec((n, d), lambda i: (0, 0)),
        ],
        out_specs=pl.BlockSpec((d, block * SUB), lambda i: (0, i)),
        out_shape=jax.ShapeDtypeStruct((d, subspaces * SUB), F32),
        scratch_shapes=[
            pltpu.VMEM((block * SUB, n), F32),
            pltpu.VMEM((d, n), BF16),
            pltpu.VMEM((d, n), BF16),
        ],
        compiler_params=pltpu.CompilerParams(vmem_limit_bytes=VMEM_BYTES),
        name="cross_terms",
    )(codes, table, points)


def bits(size):
    return size.bit_length() - 1


def partner_of(axis, bit):
    me = lax.axis_index(axis)
    mine = (me // (1 << bit)) % 2
    return mine, {axis: me + (1 - 2 * mine) * (1 << bit)}


def enter(steps):
    barrier = pltpu.get_barrier_semaphore()
    for axis, bit in steps:
        pl.semaphore_signal(barrier, inc=1, device_id=partner_of(axis, bit)[1], device_id_type=MESH)
    pl.semaphore_wait(barrier, len(steps))


def table_kernel(steps, copies, part_ref, table_ref, acc, landing, send, recv):
    chunks, height, _ = part_ref.shape
    sums = table_ref.shape[1]
    enter(steps)
    lo = 0
    half = chunks // 2
    offset = 0
    for t, (axis, bit) in enumerate(steps):
        mine, partner = partner_of(axis, bit)
        source = part_ref if t == 0 else acc
        keep = lo + mine * half
        away = lo + (1 - mine) * half
        copy = pltpu.make_async_remote_copy(
            src_ref=source.at[pl.ds(away, half)],
            dst_ref=landing.at[pl.ds(offset, half)],
            send_sem=send.at[t],
            recv_sem=recv.at[t],
            device_id=partner,
            device_id_type=MESH,
        )
        copy.start()
        copy.wait()
        acc[pl.ds(keep, half)] = source[pl.ds(keep, half)] + landing[pl.ds(offset, half)]
        lo = keep
        offset += half
        half = half // 2
    mine = acc[lo]
    pieces = []
    for i in range(sums // SUB):
        count = mine[sums + i : sums + i + 1, :] * (1.0 / copies)
        pieces.append(mine[i * SUB : (i + 1) * SUB, :] / count)
    table_ref[lo] = jnp.concatenate(pieces, axis=0)
    size = 1
    for t, (axis, bit) in enumerate(reversed(steps)):
        mine, partner = partner_of(axis, bit)
        copy = pltpu.make_async_remote_copy(
            src_ref=table_ref.at[pl.ds(lo, size)],
            dst_ref=table_ref.at[pl.ds(lo, size)],
            send_sem=send.at[len(steps) + t],
            recv_sem=recv.at[len(steps) + t],
            device_id=partner,
            device_id_type=MESH,
        )
        copy.start()
        copy.wait()
        lo = lo - mine * size
        size = size * 2


def centroid_table(sums, counts, nr, nc):
    chunks = nr * nc
    own = counts.shape[0] // chunks
    counts = counts.reshape(chunks, own, K)
    pad = -own % 8
    part = jnp.concatenate(
        [sums.reshape(chunks, own * SUB, K), jnp.pad(counts, ((0, 0), (0, pad), (0, 0)))], axis=1
    )
    steps = [("cols", b) for b in range(bits(nc))] + [("rows", b) for b in range(bits(nr))]
    vmem = pl.BlockSpec(memory_space=pltpu.VMEM)
    table = pl.pallas_call(
        functools.partial(table_kernel, steps, nc),
        in_specs=[vmem],
        out_specs=vmem,
        out_shape=jax.ShapeDtypeStruct((chunks, own * SUB, K), F32),
        scratch_shapes=[
            pltpu.VMEM(part.shape, F32),
            pltpu.VMEM(part.shape, F32),
            pltpu.SemaphoreType.DMA((2 * len(steps),)),
            pltpu.SemaphoreType.DMA((2 * len(steps),)),
        ],
        compiler_params=pltpu.CompilerParams(
            collective_id=0, has_side_effects=True, vmem_limit_bytes=VMEM_BYTES
        ),
        name="centroid_table",
    )(part)
    return table.reshape(sums.shape)


def gather_cross_kernel(row_steps, col_steps, part_ref, full_ref, acc, landing, send, recv):
    chunks = part_ref.shape[0]
    c = lax.axis_index("cols")
    enter(row_steps + col_steps)
    lo = 0
    half = chunks // 2
    offset = 0
    sem = 0
    for t, (axis, bit) in enumerate(row_steps):
        mine, partner = partner_of(axis, bit)
        source = part_ref if t == 0 else acc
        keep = lo + mine * half
        away = lo + (1 - mine) * half
        copy = pltpu.make_async_remote_copy(
            src_ref=source.at[pl.ds(away, half)],
            dst_ref=landing.at[pl.ds(offset, half)],
            send_sem=send.at[sem],
            recv_sem=recv.at[sem],
            device_id=partner,
            device_id_type=MESH,
        )
        copy.start()
        copy.wait()
        total = source[pl.ds(keep, half)] + landing[pl.ds(offset, half)]
        if half == 1:
            full_ref[c, pl.ds(keep, half)] = total
        else:
            acc[pl.ds(keep, half)] = total
        lo = keep
        offset += half
        half = half // 2
        sem += 1
    size = 1
    for axis, bit in reversed(row_steps):
        mine, partner = partner_of(axis, bit)
        block = full_ref.at[c, pl.ds(lo, size)]
        copy = pltpu.make_async_remote_copy(
            src_ref=block,
            dst_ref=block,
            send_sem=send.at[sem],
            recv_sem=recv.at[sem],
            device_id=partner,
            device_id_type=MESH,
        )
        copy.start()
        copy.wait()
        lo = lo - mine * size
        size = size * 2
        sem += 1
    held = [c]
    for axis, bit in col_steps:
        mine, partner = partner_of(axis, bit)
        copies = []
        for block in held:
            copies.append(
                pltpu.make_async_remote_copy(
                    src_ref=full_ref.at[block],
                    dst_ref=full_ref.at[block],
                    send_sem=send.at[sem],
                    recv_sem=recv.at[sem],
                    device_id=partner,
                    device_id_type=MESH,
                )
            )
            sem += 1
        for copy in copies:
            copy.start()
        for copy in copies:
            copy.wait()
        held = held + [block + (1 - 2 * mine) * (1 << bit) for block in held]


def gather_cross(part, nr, nc):
    d, width = part.shape
    part = part.reshape(nr, d // nr, width)
    row_steps = [("rows", b) for b in range(bits(nr))]
    col_steps = [("cols", b) for b in reversed(range(bits(nc)))]
    sems = 2 * len(row_steps) + nc - 1
    vmem = pl.BlockSpec(memory_space=pltpu.VMEM)
    full = pl.pallas_call(
        functools.partial(gather_cross_kernel, row_steps, col_steps),
        in_specs=[vmem],
        out_specs=vmem,
        out_shape=jax.ShapeDtypeStruct((nc,) + part.shape, F32),
        scratch_shapes=[
            pltpu.VMEM(part.shape, F32),
            pltpu.VMEM(part.shape, F32),
            pltpu.SemaphoreType.DMA((sems,)),
            pltpu.SemaphoreType.DMA((sems,)),
        ],
        compiler_params=pltpu.CompilerParams(
            collective_id=1, has_side_effects=True, vmem_limit_bytes=VMEM_BYTES
        ),
        name="gather_cross",
    )(part)
    return full.reshape(nc * d, width)


def matmul_high(left, right, dims):
    return lax.dot_general(
        left, right, dims, precision=lax.Precision.HIGH, preferred_element_type=F32
    )


def shards(nr, nc, points, codes, rotation):
    all_codes = lax.all_gather(codes, "cols", axis=0, tiled=True)
    panel = lax.all_gather(rotation, "rows", axis=0, tiled=True)
    own_rows = lax.all_to_all(panel, "cols", split_axis=0, concat_axis=1, tiled=True)
    rotated = matmul_high(own_rows, points, (((0,), (1,)), ((), ())))
    sums, counts = code_sums(all_codes, rotated)
    table = centroid_table(sums, counts, nr, nc)
    r, c = lax.axis_index("rows"), lax.axis_index("cols")
    local = codes.shape[0]
    own = lax.dynamic_slice_in_dim(table, c * local * SUB, local * SUB, 0)
    centroids = own.reshape(local, SUB, K).transpose(0, 2, 1).reshape(local, K * SUB)
    cross = gather_cross(cross_terms(all_codes, table, points), nr, nc)
    iterate = cross * (1.7 / jnp.sqrt(jnp.sum(cross * cross) + 1e-06))
    for _ in range(NS_ITERS - 1):
        gram = matmul_high(iterate, iterate, (((0,), (0,)), ((), ())))
        iterate = 1.5 * iterate - 0.5 * matmul_high(iterate, gram, (((1,), (0,)), ((), ())))
    height, width = rotation.shape
    columns = lax.dynamic_slice_in_dim(iterate, c * width, width, 1)
    rows = lax.dynamic_slice_in_dim(iterate, r * height, height, 0)
    gram = matmul_high(iterate, columns, (((0,), (0,)), ((), ())))
    block = lax.dynamic_slice_in_dim(columns, r * height, height, 0)
    block = 1.5 * block - 0.5 * matmul_high(rows, gram, (((1,), (0,)), ((), ())))
    return (block * iterate.shape[0] ** 0.5, centroids)


def solution(mesh):
    nr, nc = mesh.shape["rows"], mesh.shape["cols"]
    in_specs = (P("rows", "cols"), P("cols", "rows"), P("rows", "cols"))
    out_specs = (P("rows", "cols"), P("cols", None))
    return jax.shard_map(
        functools.partial(shards, nr, nc),
        mesh=mesh,
        in_specs=in_specs,
        out_specs=out_specs,
        check_vma=False,
    )
```

```python
import functools

import jax
import jax.numpy as jnp
from jax import lax
from jax.experimental import pallas as pl
from jax.experimental.pallas import tpu as pltpu
from jax.sharding import PartitionSpec as P

K = 256
NS_ITERS = 6
SUB = 8
LOW = 64
HIGH = K // LOW
GROUP = 4
F32 = jnp.float32
BF16 = jnp.bfloat16
MESH = pl.DeviceIdType.MESH
NT = (((1,), (1,)), ((), ()))
VMEM_BYTES = 56 * 1024 * 1024


def split(x):
    hi = x.astype(BF16)
    return hi, (x - hi.astype(F32)).astype(BF16)


def dot(left, right, dims):
    return lax.dot_general(left, right, dims, preferred_element_type=F32)


def dot3(left, right, dims):
    lh, ll = left
    rh, rl = right
    return dot(lh, rh, dims) + (dot(lh, rl, dims) + dot(ll, rh, dims))


def code_sums_kernel(codes_ref, rot_ref, sums_ref, counts_ref, left, right):
    n = codes_ref.shape[1]
    low_iota = lax.broadcasted_iota(jnp.int32, (LOW, n), 0)
    q_iota = lax.broadcasted_iota(jnp.int32, (8, n), 0)
    for g in range(codes_ref.shape[0] // GROUP):
        for i in range(GROUP):
            m = g * GROUP + i
            code = codes_ref[m : m + 1, :]
            q = code // LOW
            low = code - q * LOW
            right[i * LOW : (i + 1) * LOW, :] = jnp.where(low == low_iota, 1.0, 0.0).astype(BF16)
            value = rot_ref[m * SUB : (m + 1) * SUB, :]
            hi = value.astype(BF16).astype(F32)
            both = jnp.concatenate([hi, value - hi], axis=0)
            for h in range(HIGH):
                row = (i * HIGH + h) * 2 * SUB
                left[row : row + 2 * SUB, :] = jnp.where(q == h, both, 0.0).astype(BF16)
        for pair in range(GROUP // 2):
            row = 2 * SUB * HIGH * GROUP + pair * 16
            parts = []
            for i in range(2):
                m = g * GROUP + pair * 2 + i
                q = codes_ref[m : m + 1, :] // LOW
                parts.append(jnp.where(q == q_iota, 1.0, 0.0))
            left[row : row + 16, :] = jnp.concatenate(parts, axis=0).astype(BF16)
        out = dot(left[...], right[...], NT)
        for i in range(GROUP):
            m = g * GROUP + i
            lanes = slice(i * LOW, (i + 1) * LOW)
            pieces = []
            for h in range(HIGH):
                row = (i * HIGH + h) * 2 * SUB
                pieces.append(out[row : row + SUB, lanes] + out[row + SUB : row + 2 * SUB, lanes])
            sums_ref[m * SUB : (m + 1) * SUB, :] = jnp.concatenate(pieces, axis=1)
            row = 2 * SUB * HIGH * GROUP + i * 8
            counts_ref[m : m + 1, :] = jnp.concatenate(
                [out[row + h : row + h + 1, lanes] for h in range(HIGH)], axis=1
            )


def code_sums(codes, rot):
    subspaces, n = codes.shape
    block = 8
    rows = 2 * SUB * HIGH * GROUP + 8 * GROUP
    return pl.pallas_call(
        code_sums_kernel,
        grid=(subspaces // block,),
        in_specs=[
            pl.BlockSpec((block, n), lambda i: (i, 0)),
            pl.BlockSpec((block * SUB, n), lambda i: (i, 0)),
        ],
        out_specs=[
            pl.BlockSpec((block * SUB, K), lambda i: (i, 0)),
            pl.BlockSpec((block, K), lambda i: (i, 0)),
        ],
        out_shape=[
            jax.ShapeDtypeStruct((subspaces * SUB, K), F32),
            jax.ShapeDtypeStruct((subspaces, K), F32),
        ],
        scratch_shapes=[pltpu.VMEM((rows, n), BF16), pltpu.VMEM((GROUP * LOW, n), BF16)],
        compiler_params=pltpu.CompilerParams(vmem_limit_bytes=VMEM_BYTES),
        name="code_sums",
    )(codes, rot)


def cross_kernel(codes_ref, table_ref, points_ref, cross_ref, approx, phi, plo):
    subspaces, n = codes_ref.shape

    @pl.when(pl.program_id(0) == 0)
    def _():
        hi, lo = split(points_ref[...].T)
        phi[...] = hi
        plo[...] = lo

    for m in range(subspaces):
        rows = slice(m * SUB, (m + 1) * SUB)
        first = table_ref[rows, :128]
        second = table_ref[rows, 128:]
        for j in range(n // 128):
            lanes = slice(j * 128, (j + 1) * 128)
            code = jnp.broadcast_to(codes_ref[m : m + 1, lanes], (SUB, 128))
            inner = jnp.bitwise_and(code, 127)
            a = jnp.take_along_axis(first, inner, axis=1)
            b = jnp.take_along_axis(second, inner, axis=1)
            approx[rows, lanes] = jnp.where(code >= 128, b, a)
    cross_ref[...] = dot3((phi[...], plo[...]), split(approx[...]), NT)


def cross_terms(codes, table, points):
    subspaces, n = codes.shape
    d = points.shape[1]
    block = 32
    return pl.pallas_call(
        cross_kernel,
        grid=(subspaces // block,),
        in_specs=[
            pl.BlockSpec((block, n), lambda i: (i, 0)),
            pl.BlockSpec((block * SUB, K), lambda i: (i, 0)),
            pl.BlockSpec((n, d), lambda i: (0, 0)),
        ],
        out_specs=pl.BlockSpec((d, block * SUB), lambda i: (0, i)),
        out_shape=jax.ShapeDtypeStruct((d, subspaces * SUB), F32),
        scratch_shapes=[
            pltpu.VMEM((block * SUB, n), F32),
            pltpu.VMEM((d, n), BF16),
            pltpu.VMEM((d, n), BF16),
        ],
        compiler_params=pltpu.CompilerParams(vmem_limit_bytes=VMEM_BYTES),
        name="cross_terms",
    )(codes, table, points)


def bits(size):
    return size.bit_length() - 1


def partner_of(axis, bit):
    me = lax.axis_index(axis)
    mine = (me // (1 << bit)) % 2
    return mine, {axis: me + (1 - 2 * mine) * (1 << bit)}


def enter(steps):
    barrier = pltpu.get_barrier_semaphore()
    for axis, bit in steps:
        pl.semaphore_signal(barrier, inc=1, device_id=partner_of(axis, bit)[1], device_id_type=MESH)
    pl.semaphore_wait(barrier, len(steps))


def table_kernel(steps, copies, part_ref, table_ref, acc, landing, send, recv):
    chunks, height, _ = part_ref.shape
    sums = table_ref.shape[1]
    enter(steps)
    lo = 0
    half = chunks // 2
    offset = 0
    for t, (axis, bit) in enumerate(steps):
        mine, partner = partner_of(axis, bit)
        source = part_ref if t == 0 else acc
        keep = lo + mine * half
        away = lo + (1 - mine) * half
        copy = pltpu.make_async_remote_copy(
            src_ref=source.at[pl.ds(away, half)],
            dst_ref=landing.at[pl.ds(offset, half)],
            send_sem=send.at[t],
            recv_sem=recv.at[t],
            device_id=partner,
            device_id_type=MESH,
        )
        copy.start()
        copy.wait()
        acc[pl.ds(keep, half)] = source[pl.ds(keep, half)] + landing[pl.ds(offset, half)]
        lo = keep
        offset += half
        half = half // 2
    mine = acc[lo]
    pieces = []
    for i in range(sums // SUB):
        count = mine[sums + i : sums + i + 1, :] * (1.0 / copies)
        pieces.append(mine[i * SUB : (i + 1) * SUB, :] / count)
    table_ref[lo] = jnp.concatenate(pieces, axis=0)
    size = 1
    for t, (axis, bit) in enumerate(reversed(steps)):
        mine, partner = partner_of(axis, bit)
        copy = pltpu.make_async_remote_copy(
            src_ref=table_ref.at[pl.ds(lo, size)],
            dst_ref=table_ref.at[pl.ds(lo, size)],
            send_sem=send.at[len(steps) + t],
            recv_sem=recv.at[len(steps) + t],
            device_id=partner,
            device_id_type=MESH,
        )
        copy.start()
        copy.wait()
        lo = lo - mine * size
        size = size * 2


def centroid_table(sums, counts, nr, nc):
    chunks = nr * nc
    own = counts.shape[0] // chunks
    counts = counts.reshape(chunks, own, K)
    pad = -own % 8
    part = jnp.concatenate(
        [sums.reshape(chunks, own * SUB, K), jnp.pad(counts, ((0, 0), (0, pad), (0, 0)))], axis=1
    )
    steps = [("cols", b) for b in range(bits(nc))] + [("rows", b) for b in range(bits(nr))]
    vmem = pl.BlockSpec(memory_space=pltpu.VMEM)
    table = pl.pallas_call(
        functools.partial(table_kernel, steps, nc),
        in_specs=[vmem],
        out_specs=vmem,
        out_shape=jax.ShapeDtypeStruct((chunks, own * SUB, K), F32),
        scratch_shapes=[
            pltpu.VMEM(part.shape, F32),
            pltpu.VMEM(part.shape, F32),
            pltpu.SemaphoreType.DMA((2 * len(steps),)),
            pltpu.SemaphoreType.DMA((2 * len(steps),)),
        ],
        compiler_params=pltpu.CompilerParams(
            collective_id=0, has_side_effects=True, vmem_limit_bytes=VMEM_BYTES
        ),
        name="centroid_table",
    )(part)
    return table.reshape(sums.shape)


def remote(src, dst, send, recv, index, partner):
    return pltpu.make_async_remote_copy(
        src_ref=src,
        dst_ref=dst,
        send_sem=send.at[index],
        recv_sem=recv.at[index],
        device_id=partner,
        device_id_type=MESH,
    )


def gather_cross_kernel(parts, steps, part_ref, full_ref, acc, landing, send, recv):
    chunks = part_ref.shape[0]
    c = lax.axis_index("cols")
    enter(steps)
    sem = 0
    lows = [0] * len(parts)
    half = chunks // 2
    offset = 0
    for t in range(bits(chunks)):
        copies = []
        for i, (lanes, halving, _) in enumerate(parts):
            mine, partner = partner_of(*halving[t])
            source = part_ref if t == 0 else acc
            away = lows[i] + (1 - mine) * half
            copies.append(
                remote(
                    source.at[pl.ds(away, half), :, lanes],
                    landing.at[pl.ds(offset, half), :, lanes],
                    send,
                    recv,
                    sem,
                    partner,
                )
            )
            sem += 1
            copies[-1].start()
        for i, (lanes, halving, _) in enumerate(parts):
            mine, partner = partner_of(*halving[t])
            source = part_ref if t == 0 else acc
            keep = lows[i] + mine * half
            copies[i].wait()
            total = source[pl.ds(keep, half), :, lanes] + landing[pl.ds(offset, half), :, lanes]
            if half == 1:
                full_ref[c, pl.ds(keep, half), :, lanes] = total
            else:
                acc[pl.ds(keep, half), :, lanes] = total
            lows[i] = keep
        offset += half
        half = half // 2
    sizes = [1] * len(parts)
    held = [[c] for _ in parts]
    for t in range(len(steps)):
        copies = []
        for i, (lanes, _, doubling) in enumerate(parts):
            axis, bit = doubling[t]
            mine, partner = partner_of(axis, bit)
            for block in held[i]:
                ref = full_ref.at[block, pl.ds(lows[i], sizes[i]), :, lanes]
                copies.append(remote(ref, ref, send, recv, sem, partner))
                copies[-1].start()
                sem += 1
            if axis == "rows":
                lows[i] = lows[i] - mine * sizes[i]
                sizes[i] = sizes[i] * 2
            else:
                held[i] = held[i] + [block + (1 - 2 * mine) * (1 << bit) for block in held[i]]
        for copy in copies:
            copy.wait()


def gather_cross(part, nr, nc):
    d, width = part.shape
    part = part.reshape(nr, d // nr, width)
    rows = [("rows", b) for b in range(bits(nr))]
    cols = [("cols", b) for b in reversed(range(bits(nc)))]
    late = rows[1:] + rows[:1]
    unit = width // 8
    back, back_late = rows[::-1], late[::-1]
    parts = [
        (slice(0, 3 * unit), rows, back + cols),
        (slice(3 * unit, 6 * unit), rows, back[:-1] + cols[:1] + back[-1:] + cols[1:]),
        (slice(6 * unit, width), late, back_late[:1] + cols[:1] + back_late[1:] + cols[1:]),
    ]
    sems = 3 * (len(rows) + len(rows) * (nc // 2) + nc)
    vmem = pl.BlockSpec(memory_space=pltpu.VMEM)
    full = pl.pallas_call(
        functools.partial(gather_cross_kernel, parts, rows + cols),
        in_specs=[vmem],
        out_specs=vmem,
        out_shape=jax.ShapeDtypeStruct((nc,) + part.shape, F32),
        scratch_shapes=[
            pltpu.VMEM(part.shape, F32),
            pltpu.VMEM(part.shape, F32),
            pltpu.SemaphoreType.DMA((sems,)),
            pltpu.SemaphoreType.DMA((sems,)),
        ],
        compiler_params=pltpu.CompilerParams(
            collective_id=1, has_side_effects=True, vmem_limit_bytes=VMEM_BYTES
        ),
        name="gather_cross",
    )(part)
    return full.reshape(nc * d, width)


def reversed_bits(index, count):
    out = 0
    for b in range(count):
        out = out + ((index // (1 << b)) % 2) * (1 << (count - 1 - b))
    return out


def gather_inputs_kernel(row_steps, col_steps, rot_ref, codes_ref, rows_ref, all_codes, send, recv, own_sem):
    nr, piece, _ = rows_ref.shape
    nc = all_codes.shape[0]
    width = rot_ref.shape[1]
    r, c = lax.axis_index("rows"), lax.axis_index("cols")
    place = reversed_bits(r, len(row_steps))
    source = (c * nr + place) // nc
    is_own = source == r
    barrier = pltpu.get_barrier_semaphore()
    for j in range(nc):

        @pl.when(jnp.logical_not(is_own & (c == j)))
        def _():
            pl.semaphore_signal(barrier, inc=1, device_id=(source, j), device_id_type=MESH)

    for axis, bit in row_steps + col_steps:
        pl.semaphore_signal(barrier, inc=1, device_id=partner_of(axis, bit)[1], device_id_type=MESH)
    count = nc + len(row_steps) + len(col_steps)
    pl.semaphore_wait(barrier, jnp.where(is_own, count - 1, count))

    lanes = pl.ds(pl.multiple_of(c * width, width), width)
    partners = [partner_of(axis, bit) for axis, bit in col_steps]
    sem = 2 * nc
    first = remote(codes_ref, all_codes.at[c], send, recv, sem, partners[0][1])
    first.start()
    sem += 1
    sends = []
    for i in range(nc):
        g = r * nc + i
        to_c, to_place = g // nr, g % nr
        to_r = reversed_bits(to_place, len(row_steps))
        src = rot_ref.at[pl.ds(i * piece, piece), :]
        dst = rows_ref.at[to_place, :, lanes]
        stays = (to_c == c) & (to_r == r)
        copy = pltpu.make_async_remote_copy(
            src_ref=src,
            dst_ref=dst,
            send_sem=send.at[i],
            recv_sem=recv.at[c],
            device_id=(to_r, to_c),
            device_id_type=MESH,
        )
        sends.append((stays, copy))

        @pl.when(stays)
        def _():
            local = pltpu.make_async_copy(src, dst, own_sem)
            local.start()
            local.wait()

        @pl.when(jnp.logical_not(stays))
        def _():
            copy.start()

    all_codes[c] = codes_ref[...]
    for j in range(nc):

        @pl.when(jnp.logical_not(is_own & (c == j)))
        def _():
            ref = rows_ref.at[place, :, pl.ds(j * width, width)]
            remote(ref, ref, send, recv, j, partners[0][1]).wait_recv()

    lo, size = place, 1
    held = [c]
    mine, partner = partners[0]
    after = [c + (1 - 2 * mine) * (1 << col_steps[0][1])]
    for t, (axis, bit) in enumerate(reversed(row_steps)):
        mine, partner = partner_of(axis, bit)
        ref = rows_ref.at[pl.ds(lo, size)]
        copy = remote(ref, ref, send, recv, sem, partner)
        sem += 1
        copy.start()
        copy.wait()
        lo = lo - mine * size
        size = size * 2
    first.wait()
    held = held + after
    for (mine, partner), (axis, bit) in list(zip(partners, col_steps))[1:]:
        copies = []
        for block in held:
            ref = all_codes.at[block]
            copies.append(remote(ref, ref, send, recv, sem, partner))
            sem += 1
            copies[-1].start()
        for copy in copies:
            copy.wait()
        held = held + [block + (1 - 2 * mine) * (1 << bit) for block in held]
    for stays, copy in sends:

        @pl.when(jnp.logical_not(stays))
        def _():
            copy.wait_send()


def gather_inputs(rotation, codes, nr, nc):
    height, width = rotation.shape
    row_steps = [("rows", b) for b in range(bits(nr))]
    col_steps = [("cols", b) for b in reversed(range(bits(nc)))]
    vmem = pl.BlockSpec(memory_space=pltpu.VMEM)
    sems = 3 * nc + len(row_steps)
    rows, all_codes = pl.pallas_call(
        functools.partial(gather_inputs_kernel, row_steps, col_steps),
        in_specs=[vmem, vmem],
        out_specs=[vmem, vmem],
        out_shape=[
            jax.ShapeDtypeStruct((nr, height // nc, nc * width), F32),
            jax.ShapeDtypeStruct((nc,) + codes.shape, codes.dtype),
        ],
        scratch_shapes=[
            pltpu.SemaphoreType.DMA((sems,)),
            pltpu.SemaphoreType.DMA((sems,)),
            pltpu.SemaphoreType.DMA,
        ],
        compiler_params=pltpu.CompilerParams(
            collective_id=2, has_side_effects=True, vmem_limit_bytes=VMEM_BYTES
        ),
        name="gather_inputs",
    )(rotation, codes)
    return rows.reshape(nr * height // nc, nc * width), all_codes.reshape(-1, codes.shape[1])


def iterate_kernel(cross_ref, out_ref, hi, lo, own, landing, total, send, recv):
    size = cross_ref.shape[0]
    half = size // 2
    tile = half // 2
    mine, partner = partner_of("cols", 0)
    enter([("cols", 0)])
    band = size // 8

    total[...] = jnp.zeros_like(total)

    @pl.loop(0, 8)
    def _(i):
        x = cross_ref[pl.ds(pl.multiple_of(i * band, band), band), :]
        total[...] += jnp.sum((x * x).reshape(band // 8, 8, size), axis=0)

    scale = 1.7 / jnp.sqrt(jnp.sum(total[...], keepdims=True) + 1e-06)

    @pl.loop(0, 8)
    def _(i):
        rows = pl.ds(pl.multiple_of(i * band, band), band)
        h, l = split(cross_ref[rows, :] * scale)
        hi[rows, :] = h
        lo[rows, :] = l

    nn = (((1,), (0,)), ((), ()))

    @pl.loop(0, NS_ITERS - 1)
    def _(step):
        slot = step % 2

        def sent(t):
            rows = pl.ds(t * tile, tile)
            return pltpu.make_async_remote_copy(
                src_ref=own.at[rows, :],
                dst_ref=landing.at[slot, rows, :],
                send_sem=send.at[slot, t],
                recv_sem=recv.at[slot, t],
                device_id=partner,
                device_id_type=MESH,
            )

        for t in range(2):
            rows = pl.ds(pl.multiple_of(mine * half + t * tile, tile), tile)
            xh, xl = hi[rows, :], lo[rows, :]
            gram = dot3((xh, xl), (hi[...], lo[...]), NT)
            x = xh.astype(F32) + xl.astype(F32)
            own[t * tile : (t + 1) * tile, :] = 1.5 * x - 0.5 * dot3(
                split(gram), (hi[...], lo[...]), nn
            )
            sent(t).start()
        for t in range(2):
            rows = pl.ds(pl.multiple_of(mine * half + t * tile, tile), tile)
            h, l = split(own[t * tile : (t + 1) * tile, :])
            hi[rows, :] = h
            lo[rows, :] = l
        for t in range(2):
            rows = pl.ds(pl.multiple_of((1 - mine) * half + t * tile, tile), tile)
            sent(t).wait()
            h, l = split(landing[slot, t * tile : (t + 1) * tile, :])
            hi[rows, :] = h
            lo[rows, :] = l

    height, width = out_ref.shape
    r, c = lax.axis_index("rows"), lax.axis_index("cols")
    rows = pl.ds(pl.multiple_of(r * height, height), height)
    columns = pl.ds(pl.multiple_of(c * width, width), width)
    gram = dot3((hi[rows, :], lo[rows, :]), (hi[...], lo[...]), NT)
    x = hi[rows, columns].astype(F32) + lo[rows, columns].astype(F32)
    x = 1.5 * x - 0.5 * dot3(split(gram), (hi[:, columns], lo[:, columns]), nn)
    out_ref[...] = x * size**0.5


def new_rotation(cross, shape):
    size = cross.shape[0]
    vmem = pl.BlockSpec(memory_space=pltpu.VMEM)
    return pl.pallas_call(
        iterate_kernel,
        in_specs=[vmem],
        out_specs=vmem,
        out_shape=jax.ShapeDtypeStruct(shape, F32),
        scratch_shapes=[
            pltpu.VMEM((size, size), BF16),
            pltpu.VMEM((size, size), BF16),
            pltpu.VMEM((size // 2, size), F32),
            pltpu.VMEM((2, size // 2, size), F32),
            pltpu.VMEM((8, size), F32),
            pltpu.SemaphoreType.DMA((2, 2)),
            pltpu.SemaphoreType.DMA((2, 2)),
        ],
        compiler_params=pltpu.CompilerParams(
            collective_id=3, has_side_effects=True, vmem_limit_bytes=VMEM_BYTES
        ),
        name="new_rotation",
    )(cross)


def matmul_high(left, right, dims):
    return lax.dot_general(
        left, right, dims, precision=lax.Precision.HIGH, preferred_element_type=F32
    )


def shards(nr, nc, points, codes, rotation):
    own_rows, all_codes = gather_inputs(rotation, codes, nr, nc)
    rotated = matmul_high(own_rows, points, (((0,), (1,)), ((), ())))
    sums, counts = code_sums(all_codes, rotated)
    table = centroid_table(sums, counts, nr, nc)
    c = lax.axis_index("cols")
    local = codes.shape[0]
    own = lax.dynamic_slice_in_dim(table, c * local * SUB, local * SUB, 0)
    centroids = own.reshape(local, SUB, K).transpose(0, 2, 1).reshape(local, K * SUB)
    cross = gather_cross(cross_terms(all_codes, table, points), nr, nc)
    return (new_rotation(cross, rotation.shape), centroids)


def solution(mesh):
    nr, nc = mesh.shape["rows"], mesh.shape["cols"]
    in_specs = (P("rows", "cols"), P("cols", "rows"), P("rows", "cols"))
    out_specs = (P("rows", "cols"), P("cols", None))
    return jax.shard_map(
        functools.partial(shards, nr, nc),
        mesh=mesh,
        in_specs=in_specs,
        out_specs=out_specs,
        check_vma=False,
    )
```

```python
import functools

import jax
import jax.numpy as jnp
from jax import lax
from jax.experimental import pallas as pl
from jax.experimental.pallas import tpu as pltpu
from jax.sharding import PartitionSpec as P

K = 256
NS_ITERS = 6
SUB = 8
LOW = 64
HIGH = K // LOW
GROUP = 4
F32 = jnp.float32
BF16 = jnp.bfloat16
MESH = pl.DeviceIdType.MESH
NT = (((1,), (1,)), ((), ()))
VMEM_BYTES = 56 * 1024 * 1024


def split(x):
    hi = x.astype(BF16)
    return hi, (x - hi.astype(F32)).astype(BF16)


def dot(left, right, dims):
    return lax.dot_general(left, right, dims, preferred_element_type=F32)


def dot3(left, right, dims):
    lh, ll = left
    rh, rl = right
    return dot(lh, rh, dims) + (dot(lh, rl, dims) + dot(ll, rh, dims))


def code_sums_kernel(codes_ref, rows_ref, points_ref, part_ref, left, right, phi, plo, rotated):
    step = pl.program_id(0)
    n = codes_ref.shape[1]
    block = codes_ref.shape[0]
    own = block // part_ref.shape[0]
    panel = rows_ref.shape[1]
    turns = panel // (block * SUB)

    @pl.when(step == 0)
    def _():
        hi, lo = split(points_ref[...])
        phi[...] = hi
        plo[...] = lo

    @pl.when(step % turns == 0)
    def _():
        rotated[...] = dot3(split(rows_ref[...].T), (phi[...], plo[...]), NT)

    base = (step % turns) * (block * SUB)
    iota = lax.broadcasted_iota(jnp.int32, (16, n), 0)
    iota_16 = iota.astype(F32).astype(BF16)
    iota_8 = (iota % 8).astype(F32).astype(BF16)
    one, zero = jnp.ones((16, n), BF16), jnp.zeros((16, n), BF16)
    part_ref[...] = jnp.zeros_like(part_ref)
    for g in range(block // GROUP):
        for i in range(GROUP):
            m = g * GROUP + i
            code = jnp.broadcast_to(codes_ref[m : m + 1, :], (16, n))
            q_int = code >> bits(LOW)
            low = jnp.bitwise_and(code, LOW - 1).astype(F32).astype(BF16)
            q = q_int.astype(F32).astype(BF16)
            for k in range(LOW // 16):
                row = i * LOW + k * 16
                right[row : row + 16, :] = jnp.where(low - 16 * k == iota_16, one, zero)
            value = rotated[pl.ds(pl.multiple_of(base + m * SUB, SUB), SUB), :]
            hi = value.astype(BF16).astype(F32)
            both = jnp.concatenate([hi, value - hi], axis=0).astype(BF16)
            for h in range(HIGH):
                row = (i * HIGH + h) * 2 * SUB
                left[row : row + 2 * SUB, :] = jnp.where(q == h, both, zero)
            row = 2 * SUB * HIGH * GROUP + i * 16
            left[row : row + 16, :] = jnp.where(q == iota_8, one, zero)
        out = dot(left[...], right[...], NT)
        for i in range(GROUP):
            m = g * GROUP + i
            chunk, place = m // own, m % own
            lanes = slice(i * LOW, (i + 1) * LOW)
            pieces = []
            for h in range(HIGH):
                row = (i * HIGH + h) * 2 * SUB
                pieces.append(out[row : row + SUB, lanes] + out[row + SUB : row + 2 * SUB, lanes])
            part_ref[chunk, place * SUB : (place + 1) * SUB, :] = jnp.concatenate(pieces, axis=1)
            row = 2 * SUB * HIGH * GROUP + i * 16
            place = own * SUB + place
            part_ref[chunk, place : place + 1, :] = jnp.concatenate(
                [out[row + h : row + h + 1, lanes] for h in range(HIGH)], axis=1
            )


def code_sums(codes, own_rows, points, chunks):
    subspaces, n = codes.shape
    d = points.shape[1]
    block = 8
    own = subspaces // chunks
    panel = 256
    turns = panel // (block * SUB)
    height = own * SUB + own + -own % 8
    rows = 2 * SUB * HIGH * GROUP + 16 * GROUP
    return pl.pallas_call(
        code_sums_kernel,
        grid=(subspaces // block,),
        in_specs=[
            pl.BlockSpec((block, n), lambda i: (i, 0)),
            pl.BlockSpec((d, panel), lambda i: (0, i // turns)),
            pl.BlockSpec((n, d), lambda i: (0, 0)),
        ],
        out_specs=pl.BlockSpec((block // own, height, K), lambda i: (i, 0, 0)),
        out_shape=jax.ShapeDtypeStruct((chunks, height, K), F32),
        scratch_shapes=[
            pltpu.VMEM((rows, n), BF16),
            pltpu.VMEM((GROUP * LOW, n), BF16),
            pltpu.VMEM((n, d), BF16),
            pltpu.VMEM((n, d), BF16),
            pltpu.VMEM((panel, n), F32),
        ],
        compiler_params=pltpu.CompilerParams(vmem_limit_bytes=VMEM_BYTES),
        name="code_sums",
    )(codes, own_rows, points)


def cross_kernel(codes_ref, table_ref, points_ref, cross_ref, approx, phi, plo):
    subspaces, n = codes_ref.shape

    @pl.when(pl.program_id(0) == 0)
    def _():
        hi, lo = split(points_ref[...].T)
        phi[...] = hi
        plo[...] = lo

    for m in range(subspaces):
        rows = slice(m * SUB, (m + 1) * SUB)
        first = table_ref[rows, :128]
        second = table_ref[rows, 128:]
        for j in range(n // 128):
            lanes = slice(j * 128, (j + 1) * 128)
            code = jnp.broadcast_to(codes_ref[m : m + 1, lanes], (SUB, 128))
            inner = jnp.bitwise_and(code, 127)
            a = jnp.take_along_axis(first, inner, axis=1)
            b = jnp.take_along_axis(second, inner, axis=1)
            approx[rows, lanes] = jnp.where(code >= 128, b, a)
    cross_ref[...] = dot3((phi[...], plo[...]), split(approx[...]), NT)


def cross_terms(codes, table, points):
    subspaces, n = codes.shape
    d = points.shape[1]
    block = 32
    return pl.pallas_call(
        cross_kernel,
        grid=(subspaces // block,),
        in_specs=[
            pl.BlockSpec((block, n), lambda i: (i, 0)),
            pl.BlockSpec((block * SUB, K), lambda i: (i, 0)),
            pl.BlockSpec((n, d), lambda i: (0, 0)),
        ],
        out_specs=pl.BlockSpec((d, block * SUB), lambda i: (0, i)),
        out_shape=jax.ShapeDtypeStruct((d, subspaces * SUB), F32),
        scratch_shapes=[
            pltpu.VMEM((block * SUB, n), F32),
            pltpu.VMEM((d, n), BF16),
            pltpu.VMEM((d, n), BF16),
        ],
        compiler_params=pltpu.CompilerParams(vmem_limit_bytes=VMEM_BYTES),
        name="cross_terms",
    )(codes, table, points)


def bits(size):
    return size.bit_length() - 1


def partner_of(axis, bit):
    me = lax.axis_index(axis)
    mine = (me // (1 << bit)) % 2
    return mine, {axis: me + (1 - 2 * mine) * (1 << bit)}


def enter(steps):
    barrier = pltpu.get_barrier_semaphore()
    for axis, bit in steps:
        pl.semaphore_signal(barrier, inc=1, device_id=partner_of(axis, bit)[1], device_id_type=MESH)
    pl.semaphore_wait(barrier, len(steps))


def remote(src, dst, send, recv, index, partner):
    return pltpu.make_async_remote_copy(
        src_ref=src,
        dst_ref=dst,
        send_sem=send.at[index],
        recv_sem=recv.at[index],
        device_id=partner,
        device_id_type=MESH,
    )


def table_kernel(parts, copies, part_ref, table_ref, acc, landing, send, recv):
    chunks = part_ref.shape[0]
    sums = table_ref.shape[1]
    steps = parts[0][1]
    enter(steps)
    lows = [0] * len(parts)
    half = chunks // 2
    offset = 0
    sem = 0
    for t in range(len(steps)):
        source = part_ref if t == 0 else acc
        pending = []
        for i, (lanes, order) in enumerate(parts):
            mine, partner = partner_of(*order[t])
            away = lows[i] + (1 - mine) * half
            keep = lows[i] + mine * half
            copy = remote(
                source.at[pl.ds(away, half), :, lanes],
                landing.at[pl.ds(offset, half), :, lanes],
                send,
                recv,
                sem,
                partner,
            )
            copy.start()
            pending.append((copy, keep))
            sem += 1
        for i, (lanes, order) in enumerate(parts):
            copy, keep = pending[i]
            copy.wait()
            acc[pl.ds(keep, half), :, lanes] = (
                source[pl.ds(keep, half), :, lanes] + landing[pl.ds(offset, half), :, lanes]
            )
            lows[i] = keep
        offset += half
        half = half // 2
    for i, (lanes, order) in enumerate(parts):
        for j in range(sums // SUB):
            count = acc[lows[i], sums + j : sums + j + 1, lanes] * (1.0 / copies)
            rows = slice(j * SUB, (j + 1) * SUB)
            table_ref[lows[i], rows, lanes] = acc[lows[i], rows, lanes] / count
    size = 1
    for t in reversed(range(len(steps))):
        pending = []
        for i, (lanes, order) in enumerate(parts):
            mine, partner = partner_of(*order[t])
            ref = table_ref.at[pl.ds(lows[i], size), :, lanes]
            pending.append(remote(ref, ref, send, recv, sem, partner))
            pending[-1].start()
            lows[i] = lows[i] - mine * size
            sem += 1
        for copy in pending:
            copy.wait()
        size = size * 2


def centroid_table(part, own, nr, nc):
    chunks = nr * nc
    cols = [("cols", b) for b in range(bits(nc))]
    rows = [("rows", b) for b in range(bits(nr))]
    parts = [
        (slice(0, K // 2), cols + rows),
        (slice(K // 2, K), cols[:1] + rows[:1] + cols[1:] + rows[1:]),
    ]
    sems = 4 * (len(cols) + len(rows))
    vmem = pl.BlockSpec(memory_space=pltpu.VMEM)
    table = pl.pallas_call(
        functools.partial(table_kernel, parts, nc),
        in_specs=[vmem],
        out_specs=vmem,
        out_shape=jax.ShapeDtypeStruct((chunks, own * SUB, K), F32),
        scratch_shapes=[
            pltpu.VMEM(part.shape, F32),
            pltpu.VMEM(part.shape, F32),
            pltpu.SemaphoreType.DMA((sems,)),
            pltpu.SemaphoreType.DMA((sems,)),
        ],
        compiler_params=pltpu.CompilerParams(
            collective_id=0, has_side_effects=True, vmem_limit_bytes=VMEM_BYTES
        ),
        name="centroid_table",
    )(part)
    return table.reshape(chunks * own * SUB, K)


def gather_cross_kernel(parts, steps, part_ref, full_ref, acc, landing, send, recv):
    chunks = part_ref.shape[0]
    c = lax.axis_index("cols")
    enter(steps)
    sem = 0
    lows = [0] * len(parts)
    half = chunks // 2
    offset = 0
    for t in range(bits(chunks)):
        copies = []
        for i, (lanes, halving, _) in enumerate(parts):
            mine, partner = partner_of(*halving[t])
            source = part_ref if t == 0 else acc
            away = lows[i] + (1 - mine) * half
            copies.append(
                remote(
                    source.at[pl.ds(away, half), :, lanes],
                    landing.at[pl.ds(offset, half), :, lanes],
                    send,
                    recv,
                    sem,
                    partner,
                )
            )
            sem += 1
            copies[-1].start()
        for i, (lanes, halving, _) in enumerate(parts):
            mine, partner = partner_of(*halving[t])
            source = part_ref if t == 0 else acc
            keep = lows[i] + mine * half
            copies[i].wait()
            total = source[pl.ds(keep, half), :, lanes] + landing[pl.ds(offset, half), :, lanes]
            if half == 1:
                full_ref[c, pl.ds(keep, half), :, lanes] = total
            else:
                acc[pl.ds(keep, half), :, lanes] = total
            lows[i] = keep
        offset += half
        half = half // 2
    sizes = [1] * len(parts)
    held = [[c] for _ in parts]
    for t in range(len(steps)):
        copies = []
        for i, (lanes, _, doubling) in enumerate(parts):
            axis, bit = doubling[t]
            mine, partner = partner_of(axis, bit)
            for block in held[i]:
                ref = full_ref.at[block, pl.ds(lows[i], sizes[i]), :, lanes]
                copies.append(remote(ref, ref, send, recv, sem, partner))
                copies[-1].start()
                sem += 1
            if axis == "rows":
                lows[i] = lows[i] - mine * sizes[i]
                sizes[i] = sizes[i] * 2
            else:
                held[i] = held[i] + [block + (1 - 2 * mine) * (1 << bit) for block in held[i]]
        for copy in copies:
            copy.wait()


def gather_cross(part, nr, nc):
    d, width = part.shape
    part = part.reshape(nr, d // nr, width)
    rows = [("rows", b) for b in range(bits(nr))]
    cols = [("cols", b) for b in reversed(range(bits(nc)))]
    late = rows[1:] + rows[:1]
    unit = width // 8
    back, back_late = rows[::-1], late[::-1]
    parts = [
        (slice(0, 3 * unit), rows, back + cols),
        (slice(3 * unit, 6 * unit), rows, back[:-1] + cols[:1] + back[-1:] + cols[1:]),
        (slice(6 * unit, width), late, back_late[:1] + cols[:1] + back_late[1:] + cols[1:]),
    ]
    sems = 3 * (len(rows) + len(rows) * (nc // 2) + nc)
    vmem = pl.BlockSpec(memory_space=pltpu.VMEM)
    full = pl.pallas_call(
        functools.partial(gather_cross_kernel, parts, rows + cols),
        in_specs=[vmem],
        out_specs=vmem,
        out_shape=jax.ShapeDtypeStruct((nc,) + part.shape, F32),
        scratch_shapes=[
            pltpu.VMEM(part.shape, F32),
            pltpu.VMEM(part.shape, F32),
            pltpu.SemaphoreType.DMA((sems,)),
            pltpu.SemaphoreType.DMA((sems,)),
        ],
        compiler_params=pltpu.CompilerParams(
            collective_id=1, has_side_effects=True, vmem_limit_bytes=VMEM_BYTES
        ),
        name="gather_cross",
    )(part)
    return full.reshape(nc * d, width)


def reversed_bits(index, count):
    out = 0
    for b in range(count):
        out = out + ((index // (1 << b)) % 2) * (1 << (count - 1 - b))
    return out


def gather_inputs_kernel(row_steps, col_steps, rot_ref, codes_ref, rows_ref, all_codes, send, recv, own_sem):
    nr, piece, _ = rows_ref.shape
    nc = all_codes.shape[0]
    width = rot_ref.shape[1]
    r, c = lax.axis_index("rows"), lax.axis_index("cols")
    place = reversed_bits(r, len(row_steps))
    source = (c * nr + place) // nc
    is_own = source == r
    barrier = pltpu.get_barrier_semaphore()
    for j in range(nc):

        @pl.when(jnp.logical_not(is_own & (c == j)))
        def _():
            pl.semaphore_signal(barrier, inc=1, device_id=(source, j), device_id_type=MESH)

    for axis, bit in row_steps + col_steps:
        pl.semaphore_signal(barrier, inc=1, device_id=partner_of(axis, bit)[1], device_id_type=MESH)
    count = nc + len(row_steps) + len(col_steps)
    pl.semaphore_wait(barrier, jnp.where(is_own, count - 1, count))

    lanes = pl.ds(pl.multiple_of(c * width, width), width)
    partners = [partner_of(axis, bit) for axis, bit in col_steps]
    sem = 2 * nc
    first = remote(codes_ref, all_codes.at[c], send, recv, sem, partners[0][1])
    first.start()
    sem += 1
    sends = []
    for i in range(nc):
        g = r * nc + i
        to_c, to_place = g // nr, g % nr
        to_r = reversed_bits(to_place, len(row_steps))
        src = rot_ref.at[pl.ds(i * piece, piece), :]
        dst = rows_ref.at[to_place, :, lanes]
        stays = (to_c == c) & (to_r == r)
        copy = pltpu.make_async_remote_copy(
            src_ref=src,
            dst_ref=dst,
            send_sem=send.at[i],
            recv_sem=recv.at[c],
            device_id=(to_r, to_c),
            device_id_type=MESH,
        )
        sends.append((stays, copy))

        @pl.when(stays)
        def _():
            local = pltpu.make_async_copy(src, dst, own_sem)
            local.start()
            local.wait()

        @pl.when(jnp.logical_not(stays))
        def _():
            copy.start()

    all_codes[c] = codes_ref[...]
    for j in range(nc):

        @pl.when(jnp.logical_not(is_own & (c == j)))
        def _():
            ref = rows_ref.at[place, :, pl.ds(j * width, width)]
            remote(ref, ref, send, recv, j, partners[0][1]).wait_recv()

    lo, size = place, 1
    held = [c]
    mine, partner = partners[0]
    after = [c + (1 - 2 * mine) * (1 << col_steps[0][1])]
    for t, (axis, bit) in enumerate(reversed(row_steps)):
        mine, partner = partner_of(axis, bit)
        ref = rows_ref.at[pl.ds(lo, size)]
        copy = remote(ref, ref, send, recv, sem, partner)
        sem += 1
        copy.start()
        if t == len(row_steps) - 1:
            first.wait()
            held = held + after
            for (_, neighbour), (_, place_bit) in list(zip(partners, col_steps))[1:]:
                copies = []
                for block in held:
                    ref = all_codes.at[block]
                    copies.append(remote(ref, ref, send, recv, sem, neighbour))
                    sem += 1
                    copies[-1].start()
                for other in copies:
                    other.wait()
                side = partner_of("cols", place_bit)[0]
                held = held + [block + (1 - 2 * side) * (1 << place_bit) for block in held]
        copy.wait()
        lo = lo - mine * size
        size = size * 2
    for stays, copy in sends:

        @pl.when(jnp.logical_not(stays))
        def _():
            copy.wait_send()


def gather_inputs(rotation, codes, nr, nc):
    height, width = rotation.shape
    row_steps = [("rows", b) for b in range(bits(nr))]
    col_steps = [("cols", b) for b in reversed(range(bits(nc)))]
    vmem = pl.BlockSpec(memory_space=pltpu.VMEM)
    sems = 3 * nc + len(row_steps)
    rows, all_codes = pl.pallas_call(
        functools.partial(gather_inputs_kernel, row_steps, col_steps),
        in_specs=[vmem, vmem],
        out_specs=[vmem, vmem],
        out_shape=[
            jax.ShapeDtypeStruct((nr, height // nc, nc * width), F32),
            jax.ShapeDtypeStruct((nc,) + codes.shape, codes.dtype),
        ],
        scratch_shapes=[
            pltpu.SemaphoreType.DMA((sems,)),
            pltpu.SemaphoreType.DMA((sems,)),
            pltpu.SemaphoreType.DMA,
        ],
        compiler_params=pltpu.CompilerParams(
            collective_id=2, has_side_effects=True, vmem_limit_bytes=VMEM_BYTES
        ),
        name="gather_inputs",
    )(rotation, codes)
    return rows.reshape(nr * height // nc, nc * width), all_codes.reshape(-1, codes.shape[1])


def iterate_kernel(cross_ref, out_ref, hi, lo, own, near_gram, landing, total, send, recv):
    size = cross_ref.shape[0]
    half = size // 2
    tile = half // 2
    mine, partner = partner_of("cols", 0)
    enter([("cols", 0)])
    band = size // 8

    total[...] = jnp.zeros_like(total)

    @pl.loop(0, 8)
    def _(i):
        x = cross_ref[pl.ds(pl.multiple_of(i * band, band), band), :]
        total[...] += jnp.sum((x * x).reshape(band // 8, 8, size), axis=0)

    scale = 1.7 / jnp.sqrt(jnp.sum(total[...], keepdims=True) + 1e-06)

    @pl.loop(0, 8)
    def _(i):
        rows = pl.ds(pl.multiple_of(i * band, band), band)
        h, l = split(cross_ref[rows, :] * scale)
        hi[rows, :] = h
        lo[rows, :] = l

    nn = (((1,), (0,)), ((), ()))
    own_half = pl.ds(pl.multiple_of(mine * half, half), half)
    other_half = pl.ds(pl.multiple_of((1 - mine) * half, half), half)

    def sent(slot, t):
        rows = pl.ds(t * tile, tile)
        return pltpu.make_async_remote_copy(
            src_ref=own.at[rows, :],
            dst_ref=landing.at[slot, rows, :],
            send_sem=send.at[slot, t],
            recv_sem=recv.at[slot, t],
            device_id=partner,
            device_id_type=MESH,
        )

    def take(slot):
        for t in range(2):
            rows = pl.ds(pl.multiple_of((1 - mine) * half + t * tile, tile), tile)
            sent(slot, t).wait()
            h, l = split(landing[slot, t * tile : (t + 1) * tile, :])
            hi[rows, :] = h
            lo[rows, :] = l

    @pl.loop(0, NS_ITERS - 1)
    def _(step):
        slot = step % 2
        near = (hi[own_half, :], lo[own_half, :])
        near_gram[...] = dot3(near, near, NT)

        @pl.when(step > 0)
        def _():
            take((step + 1) % 2)

        for t in range(2):
            rows = pl.ds(pl.multiple_of(mine * half + t * tile, tile), tile)
            here = slice(t * tile, (t + 1) * tile)
            xh, xl = hi[rows, :], lo[rows, :]
            far = (hi[other_half, :], lo[other_half, :])
            far_gram = dot3((xh, xl), far, NT)
            x = xh.astype(F32) + xl.astype(F32)
            cubic = dot3(split(near_gram[here, :]), (hi[own_half, :], lo[own_half, :]), nn)
            cubic = cubic + dot3(split(far_gram), far, nn)
            own[here, :] = 1.5 * x - 0.5 * cubic
            sent(slot, t).start()
        for t in range(2):
            rows = pl.ds(pl.multiple_of(mine * half + t * tile, tile), tile)
            h, l = split(own[t * tile : (t + 1) * tile, :])
            hi[rows, :] = h
            lo[rows, :] = l

    take((NS_ITERS - 2) % 2)
    height, width = out_ref.shape
    r, c = lax.axis_index("rows"), lax.axis_index("cols")
    rows = pl.ds(pl.multiple_of(r * height, height), height)
    columns = pl.ds(pl.multiple_of(c * width, width), width)
    gram = dot3((hi[rows, :], lo[rows, :]), (hi[...], lo[...]), NT)
    x = hi[rows, columns].astype(F32) + lo[rows, columns].astype(F32)
    x = 1.5 * x - 0.5 * dot3(split(gram), (hi[:, columns], lo[:, columns]), nn)
    out_ref[...] = x * size**0.5


def new_rotation(cross, shape):
    size = cross.shape[0]
    vmem = pl.BlockSpec(memory_space=pltpu.VMEM)
    return pl.pallas_call(
        iterate_kernel,
        in_specs=[vmem],
        out_specs=vmem,
        out_shape=jax.ShapeDtypeStruct(shape, F32),
        scratch_shapes=[
            pltpu.VMEM((size, size), BF16),
            pltpu.VMEM((size, size), BF16),
            pltpu.VMEM((size // 2, size), F32),
            pltpu.VMEM((size // 2, size // 2), F32),
            pltpu.VMEM((2, size // 2, size), F32),
            pltpu.VMEM((8, size), F32),
            pltpu.SemaphoreType.DMA((2, 2)),
            pltpu.SemaphoreType.DMA((2, 2)),
        ],
        compiler_params=pltpu.CompilerParams(
            collective_id=3, has_side_effects=True, vmem_limit_bytes=VMEM_BYTES
        ),
        name="new_rotation",
    )(cross)


def shards(nr, nc, points, codes, rotation):
    own_rows, all_codes = gather_inputs(rotation, codes, nr, nc)
    chunks = nr * nc
    part = code_sums(all_codes, own_rows, points, chunks)
    table = centroid_table(part, all_codes.shape[0] // chunks, nr, nc)
    c = lax.axis_index("cols")
    local = codes.shape[0]
    own = lax.dynamic_slice_in_dim(table, c * local * SUB, local * SUB, 0)
    centroids = own.reshape(local, SUB, K).transpose(0, 2, 1).reshape(local, K * SUB)
    cross = gather_cross(cross_terms(all_codes, table, points), nr, nc)
    return (new_rotation(cross, rotation.shape), centroids)


def solution(mesh):
    nr, nc = mesh.shape["rows"], mesh.shape["cols"]
    in_specs = (P("rows", "cols"), P("cols", "rows"), P("rows", "cols"))
    out_specs = (P("rows", "cols"), P("cols", None))
    return jax.shard_map(
        functools.partial(shards, nr, nc),
        mesh=mesh,
        in_specs=in_specs,
        out_specs=out_specs,
        check_vma=False,
    )
```

```python
import functools

import jax
import jax.numpy as jnp
from jax import lax
from jax.experimental import pallas as pl
from jax.experimental.pallas import tpu as pltpu
from jax.sharding import PartitionSpec as P

K = 256
NS_ITERS = 6
SUB = 8
LOW = 64
HIGH = K // LOW
GROUP = 4
F32 = jnp.float32
BF16 = jnp.bfloat16
MESH = pl.DeviceIdType.MESH
NT = (((1,), (1,)), ((), ()))
VMEM_BYTES = 56 * 1024 * 1024


def split(x):
    hi = x.astype(BF16)
    return hi, (x - hi.astype(F32)).astype(BF16)


def dot(left, right, dims):
    return lax.dot_general(left, right, dims, preferred_element_type=F32)


def dot3(left, right, dims):
    lh, ll = left
    rh, rl = right
    return dot(lh, rh, dims) + (dot(lh, rl, dims) + dot(ll, rh, dims))


def code_sums_kernel(codes_ref, rows_ref, points_ref, part_ref, left, right, phi, plo, rotated):
    step = pl.program_id(0)
    n = codes_ref.shape[1]
    block = codes_ref.shape[0]
    own = block // part_ref.shape[0]
    panel = rows_ref.shape[1]
    turns = panel // (block * SUB)

    @pl.when(step == 0)
    def _():
        hi, lo = split(points_ref[...])
        phi[...] = hi
        plo[...] = lo

    @pl.when(step % turns == 0)
    def _():
        rotated[...] = dot3(split(rows_ref[...].T), (phi[...], plo[...]), NT)

    base = (step % turns) * (block * SUB)
    iota = lax.broadcasted_iota(jnp.int32, (16, n), 0)
    iota_16 = iota.astype(F32).astype(BF16)
    iota_8 = (iota % 8).astype(F32).astype(BF16)
    one, zero = jnp.ones((16, n), BF16), jnp.zeros((16, n), BF16)
    part_ref[...] = jnp.zeros_like(part_ref)
    for g in range(block // GROUP):
        for i in range(GROUP):
            m = g * GROUP + i
            code = jnp.broadcast_to(codes_ref[m : m + 1, :], (16, n))
            q_int = code >> bits(LOW)
            low = jnp.bitwise_and(code, LOW - 1).astype(F32).astype(BF16)
            q = q_int.astype(F32).astype(BF16)
            for k in range(LOW // 16):
                row = i * LOW + k * 16
                right[row : row + 16, :] = jnp.where(low - 16 * k == iota_16, one, zero)
            value = rotated[pl.ds(pl.multiple_of(base + m * SUB, SUB), SUB), :]
            hi = value.astype(BF16).astype(F32)
            both = jnp.concatenate([hi, value - hi], axis=0).astype(BF16)
            for h in range(HIGH):
                row = (i * HIGH + h) * 2 * SUB
                left[row : row + 2 * SUB, :] = jnp.where(q == h, both, zero)
            row = 2 * SUB * HIGH * GROUP + i * 16
            left[row : row + 16, :] = jnp.where(q == iota_8, one, zero)
        out = dot(left[...], right[...], NT)
        for i in range(GROUP):
            m = g * GROUP + i
            chunk, place = m // own, m % own
            lanes = slice(i * LOW, (i + 1) * LOW)
            pieces = []
            for h in range(HIGH):
                row = (i * HIGH + h) * 2 * SUB
                pieces.append(out[row : row + SUB, lanes] + out[row + SUB : row + 2 * SUB, lanes])
            part_ref[chunk, place * SUB : (place + 1) * SUB, :] = jnp.concatenate(pieces, axis=1)
            row = 2 * SUB * HIGH * GROUP + i * 16
            place = own * SUB + place
            part_ref[chunk, place : place + 1, :] = jnp.concatenate(
                [out[row + h : row + h + 1, lanes] for h in range(HIGH)], axis=1
            )


def code_sums(codes, own_rows, points, chunks):
    subspaces, n = codes.shape
    d = points.shape[1]
    block = 8
    own = subspaces // chunks
    panel = 256
    turns = panel // (block * SUB)
    height = own * SUB + own + -own % 8
    rows = 2 * SUB * HIGH * GROUP + 16 * GROUP
    return pl.pallas_call(
        code_sums_kernel,
        grid=(subspaces // block,),
        in_specs=[
            pl.BlockSpec((block, n), lambda i: (i, 0)),
            pl.BlockSpec((d, panel), lambda i: (0, i // turns)),
            pl.BlockSpec((n, d), lambda i: (0, 0)),
        ],
        out_specs=pl.BlockSpec((block // own, height, K), lambda i: (i, 0, 0)),
        out_shape=jax.ShapeDtypeStruct((chunks, height, K), F32),
        scratch_shapes=[
            pltpu.VMEM((rows, n), BF16),
            pltpu.VMEM((GROUP * LOW, n), BF16),
            pltpu.VMEM((n, d), BF16),
            pltpu.VMEM((n, d), BF16),
            pltpu.VMEM((panel, n), F32),
        ],
        compiler_params=pltpu.CompilerParams(vmem_limit_bytes=VMEM_BYTES),
        name="code_sums",
    )(codes, own_rows, points)


def cross_kernel(codes_ref, table_ref, points_ref, cross_ref, approx, phi, plo):
    subspaces, n = codes_ref.shape

    @pl.when(pl.program_id(0) == 0)
    def _():
        hi, lo = split(points_ref[...].T)
        phi[...] = hi
        plo[...] = lo

    for m in range(subspaces):
        rows = slice(m * SUB, (m + 1) * SUB)
        first = table_ref[rows, :128]
        second = table_ref[rows, 128:]
        for j in range(n // 128):
            lanes = slice(j * 128, (j + 1) * 128)
            code = jnp.broadcast_to(codes_ref[m : m + 1, lanes], (SUB, 128))
            inner = jnp.bitwise_and(code, 127)
            a = jnp.take_along_axis(first, inner, axis=1)
            b = jnp.take_along_axis(second, inner, axis=1)
            approx[rows, lanes] = jnp.where(code >= 128, b, a)
    cross_ref[...] = dot3((phi[...], plo[...]), split(approx[...]), NT)


def cross_terms(codes, table, points):
    subspaces, n = codes.shape
    d = points.shape[1]
    block = 32
    return pl.pallas_call(
        cross_kernel,
        grid=(subspaces // block,),
        in_specs=[
            pl.BlockSpec((block, n), lambda i: (i, 0)),
            pl.BlockSpec((block * SUB, K), lambda i: (i, 0)),
            pl.BlockSpec((n, d), lambda i: (0, 0)),
        ],
        out_specs=pl.BlockSpec((d, block * SUB), lambda i: (0, i)),
        out_shape=jax.ShapeDtypeStruct((d, subspaces * SUB), F32),
        scratch_shapes=[
            pltpu.VMEM((block * SUB, n), F32),
            pltpu.VMEM((d, n), BF16),
            pltpu.VMEM((d, n), BF16),
        ],
        compiler_params=pltpu.CompilerParams(vmem_limit_bytes=VMEM_BYTES),
        name="cross_terms",
    )(codes, table, points)


def bits(size):
    return size.bit_length() - 1


def partner_of(axis, bit):
    me = lax.axis_index(axis)
    mine = (me // (1 << bit)) % 2
    return mine, {axis: me + (1 - 2 * mine) * (1 << bit)}


def enter(steps):
    barrier = pltpu.get_barrier_semaphore()
    for axis, bit in steps:
        pl.semaphore_signal(barrier, inc=1, device_id=partner_of(axis, bit)[1], device_id_type=MESH)
    pl.semaphore_wait(barrier, len(steps))


def remote(src, dst, send, recv, index, partner):
    return pltpu.make_async_remote_copy(
        src_ref=src,
        dst_ref=dst,
        send_sem=send.at[index],
        recv_sem=recv.at[index],
        device_id=partner,
        device_id_type=MESH,
    )


def table_kernel(parts, copies, part_ref, table_ref, acc, landing, send, recv):
    chunks = part_ref.shape[0]
    sums = table_ref.shape[1]
    steps = parts[0][1]
    enter(steps)
    lows = [0] * len(parts)
    half = chunks // 2
    offset = 0
    sem = 0
    for t in range(len(steps)):
        source = part_ref if t == 0 else acc
        pending = []
        for i, (lanes, order) in enumerate(parts):
            mine, partner = partner_of(*order[t])
            away = lows[i] + (1 - mine) * half
            keep = lows[i] + mine * half
            copy = remote(
                source.at[pl.ds(away, half), :, lanes],
                landing.at[pl.ds(offset, half), :, lanes],
                send,
                recv,
                sem,
                partner,
            )
            copy.start()
            pending.append((copy, keep))
            sem += 1
        for i, (lanes, order) in enumerate(parts):
            copy, keep = pending[i]
            copy.wait()
            acc[pl.ds(keep, half), :, lanes] = (
                source[pl.ds(keep, half), :, lanes] + landing[pl.ds(offset, half), :, lanes]
            )
            lows[i] = keep
        offset += half
        half = half // 2
    for i, (lanes, order) in enumerate(parts):
        for j in range(sums // SUB):
            count = acc[lows[i], sums + j : sums + j + 1, lanes] * (1.0 / copies)
            rows = slice(j * SUB, (j + 1) * SUB)
            table_ref[lows[i], rows, lanes] = acc[lows[i], rows, lanes] / count
    size = 1
    for t in reversed(range(len(steps))):
        pending = []
        for i, (lanes, order) in enumerate(parts):
            mine, partner = partner_of(*order[t])
            ref = table_ref.at[pl.ds(lows[i], size), :, lanes]
            pending.append(remote(ref, ref, send, recv, sem, partner))
            pending[-1].start()
            lows[i] = lows[i] - mine * size
            sem += 1
        for copy in pending:
            copy.wait()
        size = size * 2


def centroid_table(part, own, nr, nc):
    chunks = nr * nc
    cols = [("cols", b) for b in range(bits(nc))]
    rows = [("rows", b) for b in range(bits(nr))]
    parts = [
        (slice(0, K // 2), cols + rows),
        (slice(K // 2, K), cols[:1] + rows[:1] + cols[1:] + rows[1:]),
    ]
    sems = 4 * (len(cols) + len(rows))
    vmem = pl.BlockSpec(memory_space=pltpu.VMEM)
    table = pl.pallas_call(
        functools.partial(table_kernel, parts, nc),
        in_specs=[vmem],
        out_specs=vmem,
        out_shape=jax.ShapeDtypeStruct((chunks, own * SUB, K), F32),
        scratch_shapes=[
            pltpu.VMEM(part.shape, F32),
            pltpu.VMEM(part.shape, F32),
            pltpu.SemaphoreType.DMA((sems,)),
            pltpu.SemaphoreType.DMA((sems,)),
        ],
        compiler_params=pltpu.CompilerParams(
            collective_id=0, has_side_effects=True, vmem_limit_bytes=VMEM_BYTES
        ),
        name="centroid_table",
    )(part)
    return table.reshape(chunks * own * SUB, K)


def gather_cross_kernel(parts, steps, part_ref, full_ref, acc, landing, send, recv):
    chunks = part_ref.shape[0]
    c = lax.axis_index("cols")
    enter(steps)
    sem = 0
    lows = [0] * len(parts)
    half = chunks // 2
    offset = 0
    for t in range(bits(chunks)):
        copies = []
        for i, (lanes, halving, _) in enumerate(parts):
            mine, partner = partner_of(*halving[t])
            source = part_ref if t == 0 else acc
            away = lows[i] + (1 - mine) * half
            copies.append(
                remote(
                    source.at[pl.ds(away, half), :, lanes],
                    landing.at[pl.ds(offset, half), :, lanes],
                    send,
                    recv,
                    sem,
                    partner,
                )
            )
            sem += 1
            copies[-1].start()
        for i, (lanes, halving, _) in enumerate(parts):
            mine, partner = partner_of(*halving[t])
            source = part_ref if t == 0 else acc
            keep = lows[i] + mine * half
            copies[i].wait()
            total = source[pl.ds(keep, half), :, lanes] + landing[pl.ds(offset, half), :, lanes]
            if half == 1:
                full_ref[c, pl.ds(keep, half), :, lanes] = total
            else:
                acc[pl.ds(keep, half), :, lanes] = total
            lows[i] = keep
        offset += half
        half = half // 2
    sizes = [1] * len(parts)
    held = [[c] for _ in parts]
    for t in range(len(steps)):
        copies = []
        for i, (lanes, _, doubling) in enumerate(parts):
            axis, bit = doubling[t]
            mine, partner = partner_of(axis, bit)
            for block in held[i]:
                ref = full_ref.at[block, pl.ds(lows[i], sizes[i]), :, lanes]
                copies.append(remote(ref, ref, send, recv, sem, partner))
                copies[-1].start()
                sem += 1
            if axis == "rows":
                lows[i] = lows[i] - mine * sizes[i]
                sizes[i] = sizes[i] * 2
            else:
                held[i] = held[i] + [block + (1 - 2 * mine) * (1 << bit) for block in held[i]]
        for copy in copies:
            copy.wait()


def gather_cross(part, nr, nc):
    d, width = part.shape
    part = part.reshape(nr, d // nr, width)
    rows = [("rows", b) for b in range(bits(nr))]
    cols = [("cols", b) for b in reversed(range(bits(nc)))]
    late = rows[1:] + rows[:1]
    unit = width // 8
    back, back_late = rows[::-1], late[::-1]
    parts = [
        (slice(0, 3 * unit), rows, back + cols),
        (slice(3 * unit, 6 * unit), rows, back[:-1] + cols[:1] + back[-1:] + cols[1:]),
        (slice(6 * unit, width), late, back_late[:1] + cols[:1] + back_late[1:] + cols[1:]),
    ]
    sems = 3 * (len(rows) + len(rows) * (nc // 2) + nc)
    vmem = pl.BlockSpec(memory_space=pltpu.VMEM)
    full = pl.pallas_call(
        functools.partial(gather_cross_kernel, parts, rows + cols),
        in_specs=[vmem],
        out_specs=vmem,
        out_shape=jax.ShapeDtypeStruct((nc,) + part.shape, F32),
        scratch_shapes=[
            pltpu.VMEM(part.shape, F32),
            pltpu.VMEM(part.shape, F32),
            pltpu.SemaphoreType.DMA((sems,)),
            pltpu.SemaphoreType.DMA((sems,)),
        ],
        compiler_params=pltpu.CompilerParams(
            collective_id=1, has_side_effects=True, vmem_limit_bytes=VMEM_BYTES
        ),
        name="gather_cross",
    )(part)
    return full.reshape(nc * d, width)


def to_place_of(index, order):
    return sum(((index // (1 << b)) % 2) * (1 << k) for k, b in enumerate(order))


def from_place(place, order):
    return sum(((place // (1 << k)) % 2) * (1 << b) for k, b in enumerate(order))


def gather_inputs_kernel(row_steps, col_steps, rot_ref, codes_ref, rows_ref, all_codes, send, recv, own_sem):
    nr, piece, _ = rows_ref.shape
    nc = all_codes.shape[0]
    width = rot_ref.shape[1]
    r, c = lax.axis_index("rows"), lax.axis_index("cols")
    row_bits = [b for _, b in row_steps]
    orders = [row_bits[::-1], row_bits[:1] + row_bits[:0:-1]]
    places = [to_place_of(r, order) for order in orders]
    sources = [(c * nr + place) // nc for place in places]
    band_of = [j * 2 // nc for j in range(nc)]
    first_band = c < nc // 2
    is_own = jnp.where(first_band, sources[0], sources[1]) == r
    barrier = pltpu.get_barrier_semaphore()
    for j in range(nc):

        @pl.when(jnp.logical_not(is_own & (c == j)))
        def _():
            pl.semaphore_signal(barrier, inc=1, device_id=(sources[band_of[j]], j), device_id_type=MESH)

    for axis, bit in row_steps + col_steps:
        pl.semaphore_signal(barrier, inc=1, device_id=partner_of(axis, bit)[1], device_id_type=MESH)
    count = nc + len(row_steps) + len(col_steps)
    pl.semaphore_wait(barrier, jnp.where(is_own, count - 1, count))

    lanes = pl.ds(pl.multiple_of(c * width, width), width)
    partners = [partner_of(axis, bit) for axis, bit in col_steps]
    sem = 2 * nc
    first = remote(codes_ref, all_codes.at[c], send, recv, sem, partners[0][1])
    first.start()
    sem += 1
    sends = []
    for i in range(nc):
        g = r * nc + i
        to_c, to_place = g // nr, g % nr
        to_r = jnp.where(
            first_band, from_place(to_place, orders[0]), from_place(to_place, orders[1])
        )
        src = rot_ref.at[pl.ds(i * piece, piece), :]
        dst = rows_ref.at[to_place, :, lanes]
        stays = (to_c == c) & (to_r == r)
        copy = pltpu.make_async_remote_copy(
            src_ref=src,
            dst_ref=dst,
            send_sem=send.at[i],
            recv_sem=recv.at[c],
            device_id=(to_r, to_c),
            device_id_type=MESH,
        )
        sends.append((stays, copy))

        @pl.when(stays)
        def _():
            local = pltpu.make_async_copy(src, dst, own_sem)
            local.start()
            local.wait()

        @pl.when(jnp.logical_not(stays))
        def _():
            copy.start()

    all_codes[c] = codes_ref[...]
    for j in range(nc):

        @pl.when(jnp.logical_not(is_own & (c == j)))
        def _():
            ref = rows_ref.at[places[band_of[j]], :, pl.ds(j * width, width)]
            remote(ref, ref, send, recv, j, partners[0][1]).wait_recv()

    lows, size = list(places), 1
    middle = rows_ref.shape[2] // 2
    bands = [slice(0, middle), slice(middle, 2 * middle)]
    held = [c]
    mine, partner = partners[0]
    after = [c + (1 - 2 * mine) * (1 << col_steps[0][1])]
    for t in range(len(row_steps)):
        moving = []
        for i in range(2):
            mine, partner = partner_of("rows", orders[i][t])
            ref = rows_ref.at[pl.ds(lows[i], size), :, bands[i]]
            moving.append(remote(ref, ref, send, recv, sem, partner))
            sem += 1
            moving[-1].start()
            lows[i] = lows[i] - mine * size
        if t == len(row_steps) - 1:
            first.wait()
            held = held + after
            for (_, neighbour), (_, place_bit) in list(zip(partners, col_steps))[1:]:
                copies = []
                for block in held:
                    ref = all_codes.at[block]
                    copies.append(remote(ref, ref, send, recv, sem, neighbour))
                    sem += 1
                    copies[-1].start()
                for other in copies:
                    other.wait()
                side = partner_of("cols", place_bit)[0]
                held = held + [block + (1 - 2 * side) * (1 << place_bit) for block in held]
        for copy in moving:
            copy.wait()
        size = size * 2
    for stays, copy in sends:

        @pl.when(jnp.logical_not(stays))
        def _():
            copy.wait_send()


def gather_inputs(rotation, codes, nr, nc):
    height, width = rotation.shape
    row_steps = [("rows", b) for b in range(bits(nr))]
    col_steps = [("cols", b) for b in reversed(range(bits(nc)))]
    vmem = pl.BlockSpec(memory_space=pltpu.VMEM)
    sems = 3 * nc + 2 * len(row_steps)
    rows, all_codes = pl.pallas_call(
        functools.partial(gather_inputs_kernel, row_steps, col_steps),
        in_specs=[vmem, vmem],
        out_specs=[vmem, vmem],
        out_shape=[
            jax.ShapeDtypeStruct((nr, height // nc, nc * width), F32),
            jax.ShapeDtypeStruct((nc,) + codes.shape, codes.dtype),
        ],
        scratch_shapes=[
            pltpu.SemaphoreType.DMA((sems,)),
            pltpu.SemaphoreType.DMA((sems,)),
            pltpu.SemaphoreType.DMA,
        ],
        compiler_params=pltpu.CompilerParams(
            collective_id=2, has_side_effects=True, vmem_limit_bytes=VMEM_BYTES
        ),
        name="gather_inputs",
    )(rotation, codes)
    return rows.reshape(nr * height // nc, nc * width), all_codes.reshape(-1, codes.shape[1])


def iterate_kernel(cross_ref, out_ref, hi, lo, own, near_gram, landing, total, send, recv):
    size = cross_ref.shape[0]
    half = size // 2
    tile = half // 2
    mine, partner = partner_of("cols", 0)
    enter([("cols", 0)])
    band = size // 8

    total[...] = jnp.zeros_like(total)

    @pl.loop(0, 8)
    def _(i):
        x = cross_ref[pl.ds(pl.multiple_of(i * band, band), band), :]
        total[...] += jnp.sum((x * x).reshape(band // 8, 8, size), axis=0)

    scale = 1.7 / jnp.sqrt(jnp.sum(total[...], keepdims=True) + 1e-06)

    @pl.loop(0, 8)
    def _(i):
        rows = pl.ds(pl.multiple_of(i * band, band), band)
        h, l = split(cross_ref[rows, :] * scale)
        hi[rows, :] = h
        lo[rows, :] = l

    nn = (((1,), (0,)), ((), ()))
    own_half = pl.ds(pl.multiple_of(mine * half, half), half)
    other_half = pl.ds(pl.multiple_of((1 - mine) * half, half), half)

    def sent(slot, t):
        rows = pl.ds(t * tile, tile)
        return pltpu.make_async_remote_copy(
            src_ref=own.at[rows, :],
            dst_ref=landing.at[slot, rows, :],
            send_sem=send.at[slot, t],
            recv_sem=recv.at[slot, t],
            device_id=partner,
            device_id_type=MESH,
        )

    def take(slot):
        for t in range(2):
            rows = pl.ds(pl.multiple_of((1 - mine) * half + t * tile, tile), tile)
            sent(slot, t).wait()
            h, l = split(landing[slot, t * tile : (t + 1) * tile, :])
            hi[rows, :] = h
            lo[rows, :] = l

    @pl.loop(0, NS_ITERS - 1)
    def _(step):
        slot = step % 2
        near = (hi[own_half, :], lo[own_half, :])
        near_gram[...] = dot3(near, near, NT)

        @pl.when(step > 0)
        def _():
            take((step + 1) % 2)

        for t in range(2):
            rows = pl.ds(pl.multiple_of(mine * half + t * tile, tile), tile)
            here = slice(t * tile, (t + 1) * tile)
            xh, xl = hi[rows, :], lo[rows, :]
            far = (hi[other_half, :], lo[other_half, :])
            far_gram = dot3((xh, xl), far, NT)
            x = xh.astype(F32) + xl.astype(F32)
            cubic = dot3(split(near_gram[here, :]), (hi[own_half, :], lo[own_half, :]), nn)
            cubic = cubic + dot3(split(far_gram), far, nn)
            own[here, :] = 1.5 * x - 0.5 * cubic
            sent(slot, t).start()
        for t in range(2):
            rows = pl.ds(pl.multiple_of(mine * half + t * tile, tile), tile)
            h, l = split(own[t * tile : (t + 1) * tile, :])
            hi[rows, :] = h
            lo[rows, :] = l

    take((NS_ITERS - 2) % 2)
    height, width = out_ref.shape
    r, c = lax.axis_index("rows"), lax.axis_index("cols")
    rows = pl.ds(pl.multiple_of(r * height, height), height)
    columns = pl.ds(pl.multiple_of(c * width, width), width)
    gram = dot3((hi[rows, :], lo[rows, :]), (hi[...], lo[...]), NT)
    x = hi[rows, columns].astype(F32) + lo[rows, columns].astype(F32)
    x = 1.5 * x - 0.5 * dot3(split(gram), (hi[:, columns], lo[:, columns]), nn)
    out_ref[...] = x * size**0.5


def new_rotation(cross, shape):
    size = cross.shape[0]
    vmem = pl.BlockSpec(memory_space=pltpu.VMEM)
    return pl.pallas_call(
        iterate_kernel,
        in_specs=[vmem],
        out_specs=vmem,
        out_shape=jax.ShapeDtypeStruct(shape, F32),
        scratch_shapes=[
            pltpu.VMEM((size, size), BF16),
            pltpu.VMEM((size, size), BF16),
            pltpu.VMEM((size // 2, size), F32),
            pltpu.VMEM((size // 2, size // 2), F32),
            pltpu.VMEM((2, size // 2, size), F32),
            pltpu.VMEM((8, size), F32),
            pltpu.SemaphoreType.DMA((2, 2)),
            pltpu.SemaphoreType.DMA((2, 2)),
        ],
        compiler_params=pltpu.CompilerParams(
            collective_id=3, has_side_effects=True, vmem_limit_bytes=VMEM_BYTES
        ),
        name="new_rotation",
    )(cross)


def shards(nr, nc, points, codes, rotation):
    own_rows, all_codes = gather_inputs(rotation, codes, nr, nc)
    chunks = nr * nc
    part = code_sums(all_codes, own_rows, points, chunks)
    table = centroid_table(part, all_codes.shape[0] // chunks, nr, nc)
    c = lax.axis_index("cols")
    local = codes.shape[0]
    own = lax.dynamic_slice_in_dim(table, c * local * SUB, local * SUB, 0)
    centroids = own.reshape(local, SUB, K).transpose(0, 2, 1).reshape(local, K * SUB)
    cross = gather_cross(cross_terms(all_codes, table, points), nr, nc)
    return (new_rotation(cross, rotation.shape), centroids)


def solution(mesh):
    nr, nc = mesh.shape["rows"], mesh.shape["cols"]
    in_specs = (P("rows", "cols"), P("cols", "rows"), P("rows", "cols"))
    out_specs = (P("rows", "cols"), P("cols", None))
    return jax.shard_map(
        functools.partial(shards, nr, nc),
        mesh=mesh,
        in_specs=in_specs,
        out_specs=out_specs,
        check_vma=False,
    )
```
